256 devices in a mesh: seq: 64 (over z, x, core), tp: 4 (over y).
Axes of the slice: x: 4, y: 4, z: 8, core: 2. Of those that a mesh axis runs over, the one named last changes fastest.
Arguments:
- queries: bfloat16 [16384, 4096], P('seq', 'tp'), may hold values from -160 to 160
- keys: bfloat16 [16384, 1024], P('seq', 'tp'), may hold values from -6 to 6
- values: bfloat16 [16384, 1024], P('seq', 'tp'), may hold values from -6 to 6
- doc_ids: int32 [16384], replicated, may hold values from 0 to 15, never falling along the last dimension, each value on 1 to 8448 neighbouring positions
- residual: bfloat16 [16384, 4096], P('seq', 'tp'), may hold values from -2 to 2
- out_weight: bfloat16 [4096, 4096], P('seq', 'tp'), may hold values from -0.09375 to 0.09375
Outputs:
- layer_out: bfloat16 [16384, 4096], P('seq', 'tp')
The draws below stay inside these ranges and needn't reach their ends.
Inputs may be any that keep to these rules, and one draw needn't show every extreme that they name: `doc_ids`: document ids never fall along the sequence; each document holds 1 to 8448 positions.
All inputs are finite; a program needn't handle non-finite values.
Results may differ from the reference program's by a relative error of at most 0.012.
Values may be sent and summed in bfloat16 or wider, within the bound.
No kernel may reach another device: no remote copies, remote signals or barrier semaphores. Data moves between devices by JAX's collectives and lax.ppermute only.
A program may use at most 320 MiB of HBM per device.

```python
import math
import jax
import jax.numpy as jnp
import numpy as np
from jax import lax

D = 4096
HEADS = 32
KV_HEADS = 8
HEAD_DIM = 128
TOKENS = 16384
DOC_COUNT = 16
DOC_MOST = 8448


def shared_keys(key):
    return jnp.clip(jax.random.normal(key, (TOKENS, KV_HEADS * HEAD_DIM), jnp.float32), -6.0, 6.0)


def draw_keys(key, part):
    base = shared_keys(key)
    return base.astype(jnp.bfloat16)


def draw_queries(key, part):
    key = jax.random.fold_in(key, 5)
    first = jax.random.fold_in(key, 0)
    drawn = jnp.clip(jax.random.normal(first, (TOKENS, HEADS * HEAD_DIM), jnp.float32), -6.0, 6.0)
    return drawn.astype(jnp.bfloat16)


def level_of(stream_key, extent, cuts, smallest, largest):
    def one(dim, blocks):
        heights = jax.random.uniform(jax.random.fold_in(jax.random.fold_in(stream_key, 6), dim), (blocks,), jnp.float32, smallest / len(cuts), largest / len(cuts))
        return jnp.repeat(jnp.exp(heights), extent[dim] // blocks).reshape((-1,) + (1,) * (len(extent) - dim - 1))

    gain = one(*cuts[0])
    for cut in cuts[1:]:
        gain = gain * one(*cut)
    return gain


def profile(amount, total, bound, lean):
    loads = [(1 << 20) // math.isqrt(grade ** lean) + 1 for grade in range(2, amount + 1)]
    spare, counts = total - bound - (amount - 1), [1] * (amount - 1)
    while spare > 0:
        free = [i for i in range(amount - 1) if counts[i] < bound]
        pool, remaining = sum([loads[i] for i in free]), spare
        for i in free:
            more = min(bound - counts[i], max(1, remaining * loads[i] // pool), spare)
            counts[i] = counts[i] + more
            spare = spare - more
    return np.array([bound] + counts)


def ragged(stream_key, amount, total, limit, skew):
    if amount == 2:
        one = jax.random.randint(stream_key, (), max(1, total - limit), min(limit, total - 1) + 1)
        return jnp.stack([one, total - one])
    lengths = jnp.asarray(profile(amount, total, limit, skew), jnp.int32)
    couples = (amount - 1) // 2
    source_of, sink = lengths[1:1 + 2 * couples:2], lengths[2:2 + 2 * couples:2]
    margin = jnp.minimum(source_of - 1, limit - sink)
    shifted = jax.random.randint(jax.random.fold_in(stream_key, 1), (couples,), 0, 1 << 20) % (margin + 1)
    lengths = lengths.at[1:1 + 2 * couples:2].set(source_of - shifted).at[2:2 + 2 * couples:2].set(sink + shifted)
    return lengths[jax.random.permutation(jax.random.fold_in(stream_key, 2), amount)]


def centred(rng, extent, width, limit, shards=(), kind=jnp.bfloat16):
    entries = jax.random.normal(rng, extent, jnp.float32) * width
    if len(shards) > 0:
        entries = level_of(rng, extent, shards, -0.22, 0.18) * entries
    return jnp.clip(entries, min=-limit, max=limit).astype(kind)


def setup_inputs(seed: int = 0) -> dict:
    streams_of = jax.random.split(jax.random.key(seed), 7)
    queries = draw_queries(jax.random.fold_in(streams_of[6], 71), 0)
    keys = draw_keys(jax.random.fold_in(streams_of[6], 71), 0)
    values = centred(streams_of[2], (TOKENS, KV_HEADS * HEAD_DIM), 1.0, 6.0, ((0, 64), (1, 4)))
    doc_ids = jnp.searchsorted(jnp.cumsum(ragged(streams_of[3], DOC_COUNT, TOKENS, DOC_MOST, 2)), jnp.arange(TOKENS), side="right").astype(jnp.int32)
    residual = centred(streams_of[4], (TOKENS, D), 0.3, 2.0, ((0, 64), (1, 4)))
    out_weight = centred(streams_of[5], (D, HEADS * HEAD_DIM), (HEADS * HEAD_DIM) ** -0.5, 0.09375, ((0, 64), (1, 4)))
    return {"queries": queries, "keys": keys, "values": values, "doc_ids": doc_ids, "residual": residual, "out_weight": out_weight}


def reference(queries, keys, values, doc_ids, residual, out_weight):
    scale = HEAD_DIM ** -0.5
    groups = HEADS // KV_HEADS
    block = min(1024, TOKENS)
    pieces = []
    for index in range(TOKENS // block):
        begin = index * block
        end = begin + block
        q_block = queries[begin:end].reshape(block, KV_HEADS, groups, HEAD_DIM).transpose(1, 0, 2, 3)
        k_block = keys[:end].reshape(end, KV_HEADS, HEAD_DIM).transpose(1, 0, 2)
        v_block = values[:end].reshape(end, KV_HEADS, HEAD_DIM).transpose(1, 0, 2)
        q_pos = jnp.arange(begin, end, dtype=jnp.int32)
        k_pos = jnp.arange(0, end, dtype=jnp.int32)
        visible = (k_pos[None, :] <= q_pos[:, None]) & (doc_ids[:end][None, :] == doc_ids[begin:end][:, None])

        def one_head(operands):
            q_head, k_head, v_head = operands
            scores = jnp.einsum("rgd,pd->grp", q_head.astype(jnp.float32), k_head.astype(jnp.float32)) * scale
            scores = jnp.where(visible[None], scores, -1e30)
            top = jnp.max(scores, axis=2, keepdims=True)
            weights = jnp.where(visible[None], jnp.exp(scores - top), 0.0)
            total = jnp.sum(weights, axis=2)
            probs = lax.optimization_barrier(weights.astype(jnp.bfloat16))
            summed = jnp.einsum("grp,pd->rgd", probs.astype(jnp.float32), v_head.astype(jnp.float32))
            return (summed / total.T[:, :, None]).astype(jnp.bfloat16)

        heads_out = lax.map(one_head, (q_block, k_block, v_block))
        pieces.append(heads_out.transpose(1, 0, 2, 3).reshape(block, HEADS * HEAD_DIM))
    attended = jnp.concatenate(pieces, axis=0)
    projected = lax.dot_general(attended, out_weight, (((1,), (1,)), ((), ())), preferred_element_type=jnp.float32)
    return (residual.astype(jnp.float32) + projected).astype(jnp.bfloat16)
```

```python
import functools
import math

import jax
import jax.numpy as jnp
from jax import lax
from jax.experimental import pallas as pl
from jax.experimental.pallas import tpu as pltpu
from jax.sharding import Mesh, PartitionSpec as P

HEADS = 32
KV_HEADS = 8
HEAD_DIM = 128
GROUPS = HEADS // KV_HEADS
EXPONENT_SCALE = HEAD_DIM ** -0.5 * math.log2(math.e)
HIDDEN = -1e30
Z, X, CORES, TP = 8, 4, 2, 4
BACK = 4


def attend_kernel(sizes, first, last, row_tile, info, lo_ref, q_ref, *refs):
    count = len(sizes)
    blocks = refs[:count]
    refs = refs[count:]
    if not first:
        acc_in, top_in = refs[:2]
        refs = refs[2:]
    if last:
        out_ref = refs[0]
        refs = refs[1:]
    acc, top, value_ones = refs
    rows = q_ref.shape[0]
    if first:
        acc[...] = jnp.zeros_like(acc)
        top[...] = jnp.full_like(top, HIDDEN)
    else:
        acc[...] = acc_in[...]
        top[...] = top_in[...]
    value_ones[:, HEAD_DIM:] = jnp.ones((value_ones.shape[0], HEAD_DIM), jnp.bfloat16)
    row0 = info[0]
    lo_min = info[1]
    lo_max = info[2]
    for b in range(count):
        n = sizes[b]
        block = blocks[b]
        start = info[3 + b]
        end = start + n - 1
        seen = (start >= 0) & (start <= row0 + rows - 1) & (end >= lo_min)
        whole = (end <= row0) & (start >= lo_max)

        def work(masked, n=n, block=block, start=start):
            value_ones[:n, :HEAD_DIM] = block[:, HEAD_DIM:]
            for r in range(0, rows, row_tile):
                tile = pl.ds(r, row_tile)
                if masked:
                    col = start + lax.broadcasted_iota(jnp.int32, (row_tile, n), 1)
                    row = row0 + r + lax.broadcasted_iota(jnp.int32, (row_tile, n), 0)
                    visible = (col <= row) & (col >= lo_ref[tile, :])
                for g in range(GROUPS):
                    scores = lax.dot_general(
                        q_ref[tile, pl.ds(g * HEAD_DIM, HEAD_DIM)],
                        block[:, :HEAD_DIM],
                        (((1,), (1,)), ((), ())),
                        preferred_element_type=jnp.float32,
                    )
                    if masked:
                        scores = jnp.where(visible, scores, HIDDEN)
                    old = top[g, tile, :]
                    new = jnp.maximum(old, jnp.max(scores, axis=1, keepdims=True))
                    top[g, tile, :] = new
                    wide = jnp.concatenate([new] * (n // HEAD_DIM), axis=1)
                    weights = jnp.exp2((scores - wide) * EXPONENT_SCALE)
                    if masked:
                        weights = jnp.where(visible, weights, 0.0)
                    fade = jnp.exp2((old - new) * EXPONENT_SCALE)
                    summed = jnp.dot(
                        weights.astype(jnp.bfloat16),
                        value_ones[:n, :],
                        preferred_element_type=jnp.float32,
                    )
                    acc[g, tile, :] = acc[g, tile, :] * jnp.concatenate([fade, fade], axis=1) + summed

        pl.when(seen & whole)(functools.partial(work, False))
        pl.when(seen & jnp.logical_not(whole))(functools.partial(work, True))
    if last:
        for g in range(GROUPS):
            out_ref[:, pl.ds(g * HEAD_DIM, HEAD_DIM)] = (
                acc[g, :, :HEAD_DIM] / acc[g, :, HEAD_DIM:]
            ).astype(jnp.bfloat16)


def attend(info, lo, q, blocks, state, last, row_tile=256):
    rows = q.shape[0]
    sizes = tuple(b.shape[0] for b in blocks)
    first = state is None
    vmem = pl.BlockSpec(memory_space=pltpu.VMEM)
    acc = jax.ShapeDtypeStruct((GROUPS, rows, 2 * HEAD_DIM), jnp.float32)
    top = jax.ShapeDtypeStruct((GROUPS, rows, HEAD_DIM), jnp.float32)
    scratch = [pltpu.VMEM((max(sizes), 2 * HEAD_DIM), jnp.bfloat16)]
    if last:
        out = jax.ShapeDtypeStruct((rows, GROUPS * HEAD_DIM), jnp.bfloat16)
        out_specs = vmem
        scratch = [pltpu.VMEM(acc.shape, acc.dtype), pltpu.VMEM(top.shape, top.dtype)] + scratch
    else:
        out = (acc, top)
        out_specs = (vmem, vmem)
    args = [info, lo, q, *blocks] + ([] if first else list(state))
    keys = sum(sizes)
    return pl.pallas_call(
        functools.partial(attend_kernel, sizes, first, last, row_tile),
        out_shape=out,
        out_specs=out_specs,
        in_specs=[pl.BlockSpec(memory_space=pltpu.SMEM)] + [vmem] * (len(args) - 1),
        scratch_shapes=scratch,
        compiler_params=pltpu.CompilerParams(vmem_limit_bytes=48 << 20),
        cost_estimate=pl.CostEstimate(
            flops=4 * rows * GROUPS * keys * HEAD_DIM,
            bytes_accessed=8 << 20,
            transcendentals=rows * GROUPS * keys,
        ),
        name="attend",
    )(*args)


def ring(n, step):
    return [(i, (i + step) % n) for i in range(n)]


def local(queries, keys, values, doc_ids, residual, out_weight):
    tokens = queries.shape[0]
    rows = CORES * tokens
    half = queries.shape[1] // 2
    core = lax.axis_index("core")
    z = lax.axis_index("z")
    x = lax.axis_index("x")
    chip = z * X + x
    row0 = chip * rows
    is0 = core == 0

    weight = lax.all_gather(out_weight, ("z", "x", "core"), axis=0, tiled=True)

    swap = [(0, 1), (1, 0)]

    def head_split(mine0, mine1):
        kept = jnp.where(is0, mine0, mine1)
        sent = jnp.where(is0, mine1, mine0)
        got = lax.ppermute(sent, "core", swap)
        return jnp.where(
            is0, jnp.concatenate([kept, got], axis=0), jnp.concatenate([got, kept], axis=0)
        )

    def kv_of(h):
        cols = slice(h * HEAD_DIM, (h + 1) * HEAD_DIM)
        return jnp.concatenate([keys[:, cols], values[:, cols]], axis=1)

    kv = head_split(kv_of(0), kv_of(1))
    q = head_split(queries[:, :half], queries[:, half:])

    begins = jnp.sum(
        (doc_ids[None, :] < jnp.arange(16, dtype=jnp.int32)[:, None]).astype(jnp.int32), axis=1
    )
    own_docs = lax.dynamic_slice_in_dim(doc_ids, row0, rows)
    lo = jnp.sum(
        jnp.where(own_docs[:, None] == jnp.arange(16, dtype=jnp.int32)[None, :], begins[None, :], 0),
        axis=1,
    )

    def begin_of(k, dx, shift=0):
        zz = z - k
        return jnp.where(zz >= 0, (zz * X + (x + dx) % X) * rows + shift, -1)

    held = kv
    state = None
    hop = rows // 2
    attended = None
    for k in range(BACK + 1):
        if k == 0:
            left = [(0, 1), (1, 2), (2, 3)]
            right = [(0, 3), (1, 0)]
            far_left = [(1, 2), (2, 3)]
            far_right = [(3, 2), (0, 3)]
        elif k == BACK:
            left = ring(X, 1)
            right = [(1, 0), (2, 1), (3, 2)]
            far_left = [(3, 0), (0, 1)]
            far_right = [(1, 0), (2, 1)]
        else:
            left, right = ring(X, 1), ring(X, -1)
            far_left, far_right = left, right
        if k > 0:
            held = lax.ppermute(held, "z", [(i, i + 1) for i in range(k - 1, Z - 1)])
        from_left = lax.ppermute(held, "x", left)
        from_right = lax.ppermute(held, "x", right)
        far_lo = lax.ppermute(from_left[:hop], "x", far_left)
        far_hi = lax.ppermute(from_right[hop:], "x", far_right)
        blocks = [held, from_left, from_right, far_lo, far_hi]
        begins_at = [
            begin_of(k, 0), begin_of(k, -1), begin_of(k, 1), begin_of(k, 2), begin_of(k, 2, hop),
        ]
        if k == BACK:
            tail = lax.ppermute(
                held[hop:],
                ("z", "x"),
                [(i * X + X - 1, (i + 1) * X) for i in range(BACK, Z - 1)],
            )
            blocks.append(tail)
            begins_at.append(
                jnp.where((x == 0) & (z > BACK), row0 - (X * BACK + 1) * rows + hop, -1)
            )
        info = jnp.stack([row0, lo[0], lo[rows - 1]] + begins_at).astype(jnp.int32)
        state = attend(info, lo[:, None], q, blocks, state, k == BACK)
    attended = state

    kept = jnp.where(is0, attended[:tokens], attended[tokens:])
    sent = jnp.where(is0, attended[tokens:], attended[:tokens])
    got = lax.ppermute(sent, "core", swap)
    attended = jnp.where(
        is0, jnp.concatenate([kept, got], axis=1), jnp.concatenate([got, kept], axis=1)
    )
    partial_out = lax.dot_general(
        attended, weight, (((1,), (1,)), ((), ())), preferred_element_type=jnp.float32
    )
    mixed = lax.psum_scatter(
        partial_out.astype(jnp.bfloat16), "tp", scatter_dimension=1, tiled=True
    ).astype(jnp.float32)
    return (residual.astype(jnp.float32) + mixed).astype(jnp.bfloat16)


def solution(mesh):
    mesh = Mesh(mesh.devices.reshape(Z, X, CORES, TP), ("z", "x", "core", "tp"))
    tile = P(("z", "x", "core"), "tp")
    return jax.shard_map(
        local,
        mesh=mesh,
        in_specs=(tile, tile, tile, P(), tile, tile),
        out_specs=tile,
        check_vma=False,
    )
```

```python
import functools
import math

import jax
import jax.numpy as jnp
from jax import lax
from jax.experimental import pallas as pl
from jax.experimental.pallas import tpu as pltpu
from jax.sharding import Mesh, PartitionSpec as P

HEADS = 32
KV_HEADS = 8
HEAD_DIM = 128
GROUPS = HEADS // KV_HEADS
EXPONENT_SCALE = HEAD_DIM ** -0.5 * math.log2(math.e)
HIDDEN = -1e30
Z, X, CORES, TP = 8, 4, 2, 4
BACK = 4
UNROLL = 2


def attend_kernel(sizes, base, causal_chunks, first, last, info, lo_ref, q_ref, *refs):
    count = len(sizes)
    blocks = refs[:count]
    refs = refs[count:]
    if not first:
        acc_in, top_in = refs[:2]
        refs = refs[2:]
    if last:
        out_ref = refs[0]
        refs = refs[1:]
    acc, top, key_buf, value_ones = refs
    rows = q_ref.shape[0]
    total = sum(sizes)
    if first:
        acc[...] = jnp.zeros_like(acc)
        top[...] = jnp.full_like(top, HIDDEN)
    else:
        acc[...] = acc_in[...]
        top[...] = top_in[...]
    value_ones[:, HEAD_DIM:] = jnp.ones((total, HEAD_DIM), jnp.bfloat16)
    at = 0
    for b in range(count):
        span = pl.ds(at, sizes[b])
        key_buf[span, :] = blocks[b][:, :HEAD_DIM]
        value_ones[span, :HEAD_DIM] = blocks[b][:, HEAD_DIM:]
        at += sizes[b]
    row0 = info[0]
    lo_min = info[1]
    lo_max = info[2]

    def seen(start, n):
        return (start >= 0) & (start <= row0 + rows - 1) & (start + n - 1 >= lo_min)

    def whole(start, n):
        return (start >= lo_max) & (start + n - 1 <= row0)

    def work(keys, width, starts, masked, causal=False):
        def step(t, _):
            k = key_buf[keys, :]
            v = value_ones[keys, :]
            if masked:
                each = width // len(starts)
                lane = lax.broadcasted_iota(jnp.int32, (1, width), 1)
                col = starts[0] + lane
                for i in range(1, len(starts)):
                    col = jnp.where(lane >= i * each, starts[i] + lane - i * each, col)
                visible = col >= lo_ref[...]
                if causal:
                    row = row0 + lax.broadcasted_iota(jnp.int32, (rows, 1), 0)
                    visible = visible & (col <= row)
            scores = []
            for u in range(UNROLL):
                q = q_ref[:, pl.ds(pl.multiple_of((t * UNROLL + u) * HEAD_DIM, HEAD_DIM), HEAD_DIM)]
                s = lax.dot_general(
                    q, k, (((1,), (1,)), ((), ())), preferred_element_type=jnp.float32
                )
                scores.append(jnp.where(visible, s, HIDDEN) if masked else s)
            for u in range(UNROLL):
                g = t * UNROLL + u
                s = scores[u]
                old = top[g]
                new = jnp.maximum(old, jnp.max(s, axis=1, keepdims=True))
                top[g] = new
                wide = jnp.concatenate([new] * (width // HEAD_DIM), axis=1)
                weights = jnp.exp2((s - wide) * EXPONENT_SCALE)
                fade = jnp.exp2((old - new) * EXPONENT_SCALE)
                summed = jnp.dot(
                    weights.astype(jnp.bfloat16), v, preferred_element_type=jnp.float32
                )
                acc[g] = acc[g] * jnp.concatenate([fade, fade], axis=1) + summed
            return 0

        lax.fori_loop(0, GROUPS // UNROLL, step, 0)

    def chunk(causal, j, _):
        one = info[base + 2 * j]
        two = info[base + 2 * j + 1]
        keys = pl.ds(pl.multiple_of(j * 2 * rows, 2 * rows), 2 * rows)
        any_seen = seen(one, rows) | seen(two, rows)
        both = whole(one, rows) & whole(two, rows)
        pl.when(any_seen & both)(lambda: work(keys, 2 * rows, [one], False))
        pl.when(any_seen & jnp.logical_not(both))(
            lambda: work(keys, 2 * rows, [one, two], True, causal)
        )
        return 0

    pairs = total // (2 * rows)
    if causal_chunks:
        lax.fori_loop(0, causal_chunks, functools.partial(chunk, True), 0)
    lax.fori_loop(causal_chunks, pairs, functools.partial(chunk, False), 0)
    extra = total - pairs * 2 * rows
    if extra:
        start = info[base + 2 * pairs]
        pl.when(seen(start, extra))(
            lambda: work(pl.ds(pairs * 2 * rows, extra), extra, [start], True)
        )
    if last:
        for g in range(GROUPS):
            out_ref[:, pl.ds(g * HEAD_DIM, HEAD_DIM)] = (
                acc[g, :, :HEAD_DIM] / acc[g, :, HEAD_DIM:]
            ).astype(jnp.bfloat16)


def attend(info, lo, q, blocks, state, base, causal_chunks, last):
    rows = q.shape[0]
    sizes = tuple(b.shape[0] for b in blocks)
    total = sum(sizes)
    first = state is None
    vmem = pl.BlockSpec(memory_space=pltpu.VMEM)
    acc = jax.ShapeDtypeStruct((GROUPS, rows, 2 * HEAD_DIM), jnp.float32)
    top = jax.ShapeDtypeStruct((GROUPS, rows, HEAD_DIM), jnp.float32)
    scratch = [
        pltpu.VMEM((total, HEAD_DIM), jnp.bfloat16),
        pltpu.VMEM((total, 2 * HEAD_DIM), jnp.bfloat16),
    ]
    if last:
        out = jax.ShapeDtypeStruct((rows, GROUPS * HEAD_DIM), jnp.bfloat16)
        out_specs = vmem
        scratch = [pltpu.VMEM(acc.shape, acc.dtype), pltpu.VMEM(top.shape, top.dtype)] + scratch
    else:
        out = (acc, top)
        out_specs = (vmem, vmem)
    args = [info, lo, q, *blocks] + ([] if first else list(state))
    return pl.pallas_call(
        functools.partial(attend_kernel, sizes, base, causal_chunks, first, last),
        out_shape=out,
        out_specs=out_specs,
        in_specs=[pl.BlockSpec(memory_space=pltpu.SMEM)] + [vmem] * (len(args) - 1),
        scratch_shapes=scratch,
        compiler_params=pltpu.CompilerParams(vmem_limit_bytes=24 << 20),
        cost_estimate=pl.CostEstimate(
            flops=4 * rows * GROUPS * total * HEAD_DIM,
            bytes_accessed=8 << 20,
            transcendentals=rows * GROUPS * total,
        ),
        name="attend",
    )(*args)


def ring(n, step):
    return [(i, (i + step) % n) for i in range(n)]


def local(queries, keys, values, doc_ids, residual, out_weight):
    tokens = queries.shape[0]
    rows = CORES * tokens
    half = queries.shape[1] // 2
    core = lax.axis_index("core")
    z = lax.axis_index("z")
    x = lax.axis_index("x")
    chip = z * X + x
    row0 = chip * rows
    is0 = core == 0

    swap = [(0, 1), (1, 0)]
    y = lax.axis_index("tp")

    def head_split(mine0, mine1):
        kept = jnp.where(is0, mine0, mine1)
        sent = jnp.where(is0, mine1, mine0)
        got = lax.ppermute(sent, "core", swap)
        return jnp.where(
            is0, jnp.concatenate([kept, got], axis=0), jnp.concatenate([got, kept], axis=0)
        )

    def kv_of(h):
        cols = slice(h * HEAD_DIM, (h + 1) * HEAD_DIM)
        return jnp.concatenate([keys[:, cols], values[:, cols]], axis=1)

    kv = head_split(kv_of(0), kv_of(1))
    q = head_split(queries[:, :half], queries[:, half:])

    begins = jnp.sum(
        (doc_ids[None, :] < jnp.arange(16, dtype=jnp.int32)[:, None]).astype(jnp.int32), axis=1
    )
    own_docs = lax.dynamic_slice_in_dim(doc_ids, row0, rows)
    lo = jnp.sum(
        jnp.where(own_docs[:, None] == jnp.arange(16, dtype=jnp.int32)[None, :], begins[None, :], 0),
        axis=1,
    )

    spots = jnp.arange(4 * (BACK + 1), dtype=jnp.int32)
    back = z - spots // 4
    aside = jnp.where(spots % 4 == 3, 2, spots % 4 + jnp.where(spots % 4 == 1, 2, 0))
    aside = jnp.where(spots % 4 == 2, 1, aside)
    starts = jnp.where(back >= 0, (back * X + (x + aside) % X) * rows, -1)
    tail_start = jnp.where(
        (x == 0) & (z > BACK), row0 - (X * BACK + 1) * rows + rows // 2, -1
    )
    info = jnp.concatenate(
        [jnp.stack([row0, lo[0], lo[rows - 1]]), starts, tail_start[None]]
    ).astype(jnp.int32)

    def forward(block, step, low):
        return lax.ppermute(block, "z", [(i, i + step) for i in range(low, Z - step)])

    def from_sides(block, left, right, far):
        return [
            lax.ppermute(block, "x", left),
            lax.ppermute(block, "x", right),
            lax.ppermute(block, "x", far),
        ]

    full = (ring(X, 1), ring(X, -1), ring(X, 2))
    pieces = [out_weight] + from_sides(out_weight, *full)
    weight = jnp.stack(
        [
            jnp.where(
                j == x,
                pieces[0],
                jnp.where(
                    j == (x + 3) % X,
                    pieces[1],
                    jnp.where(j == (x + 1) % X, pieces[2], pieces[3]),
                ),
            )
            for j in range(X)
        ]
    )
    weight = lax.all_gather(weight, "z", axis=0, tiled=False)

    lo_col = lo[:, None]
    held = kv
    blocks = None
    state = None
    for k in range(BACK + 1):
        if k == 0:
            pairs = ([(0, 1), (1, 2), (2, 3)], [(0, 3)], [(0, 2), (1, 3)])
        elif k == BACK:
            pairs = (ring(X, 1), [(1, 0), (2, 1), (3, 2)], [(2, 0), (3, 1)])
        else:
            pairs = full
        ahead = forward(held, 1, k) if k < BACK else None
        coming = [held] + from_sides(held, *pairs)
        if k == BACK:
            coming.append(
                lax.ppermute(
                    held[rows // 2 :],
                    ("z", "x"),
                    [(i * X + X - 1, (i + 1) * X) for i in range(BACK, Z - 1)],
                )
            )
        if k > 0:
            state = attend(
                info, lo_col, q, blocks, state, 3 + 4 * (k - 1), 2 if k == 1 else 0, False
            )
        if k < BACK:
            ahead, coming, state = lax.optimization_barrier((ahead, coming, state))
        held, blocks = ahead, coming
    state = attend(info, lo_col, q, blocks, state, 3 + 4 * BACK, 0, True)
    attended = state

    other = lax.ppermute(attended, "core", swap)
    attended = jnp.where(
        is0,
        jnp.concatenate([attended, other], axis=1),
        jnp.concatenate([other, attended], axis=1),
    )

    def share(d):
        block = lax.dynamic_slice_in_dim(weight, ((y + d) % TP) * 2, 2, axis=0)
        return lax.dot_general(
            attended,
            block.reshape(-1, out_weight.shape[1]),
            (((1,), (1,)), ((), ())),
            preferred_element_type=jnp.float32,
        )

    got = [
        lax.ppermute(share(d).astype(jnp.bfloat16), "tp", ring(TP, d)) for d in (2, 1, 3)
    ]
    mixed = share(0)
    for part in got:
        mixed = mixed + part.astype(jnp.float32)
    kept = jnp.where(is0, mixed[:tokens], mixed[tokens:])
    sent = jnp.where(is0, mixed[tokens:], mixed[:tokens]).astype(jnp.bfloat16)
    given = lax.ppermute(sent, "core", swap).astype(jnp.float32)
    even = jnp.where(is0, kept, given).reshape(tokens, -1, out_weight.shape[0])
    odd = jnp.where(is0, given, kept).reshape(tokens, -1, out_weight.shape[0])
    mixed = jnp.stack([even, odd], axis=2).reshape(residual.shape)
    return (residual.astype(jnp.float32) + mixed).astype(jnp.bfloat16)


def solution(mesh):
    mesh = Mesh(mesh.devices.reshape(Z, X, CORES, TP), ("z", "x", "core", "tp"))
    tile = P(("z", "x", "core"), "tp")
    return jax.shard_map(
        local,
        mesh=mesh,
        in_specs=(tile, tile, tile, P(), tile, tile),
        out_specs=tile,
        check_vma=False,
    )
```

```python
import functools
import math

import jax
import jax.numpy as jnp
from jax import lax
from jax.experimental import pallas as pl
from jax.experimental.pallas import tpu as pltpu
from jax.sharding import Mesh, PartitionSpec as P

HEADS = 32
KV_HEADS = 8
HEAD_DIM = 128
GROUPS = HEADS // KV_HEADS
EXPONENT_SCALE = HEAD_DIM ** -0.5 * math.log2(math.e)
HIDDEN = -1e30
Z, X, CORES, TP = 8, 4, 2, 4
BACK = 4
UNROLL = 2


def attend_kernel(sizes, base, causal_chunks, first, last, info, lo_ref, q_ref, *refs):
    count = len(sizes)
    blocks = refs[:count]
    refs = refs[count:]
    if not first:
        acc_in, top_in = refs[:2]
        refs = refs[2:]
    if last:
        out_ref = refs[0]
        refs = refs[1:]
    acc, top, key_buf, value_ones = refs
    rows = q_ref.shape[0]
    total = sum(sizes)
    if first:
        acc[...] = jnp.zeros_like(acc)
        top[...] = jnp.full_like(top, HIDDEN)
    else:
        acc[...] = acc_in[...]
        top[...] = top_in[...]
    value_ones[:, HEAD_DIM:] = jnp.ones((total, HEAD_DIM), jnp.bfloat16)
    at = 0
    for b in range(count):
        span = pl.ds(at, sizes[b])
        key_buf[span, :] = blocks[b][:, :HEAD_DIM]
        value_ones[span, :HEAD_DIM] = blocks[b][:, HEAD_DIM:]
        at += sizes[b]
    row0 = info[0]
    lo_min = info[1]
    lo_max = info[2]

    def seen(start, n):
        return (start >= 0) & (start <= row0 + rows - 1) & (start + n - 1 >= lo_min)

    def whole(start, n):
        return (start >= lo_max) & (start + n - 1 <= row0)

    def work(keys, width, starts, masked, causal=False):
        def step(t, _):
            k = key_buf[keys, :]
            v = value_ones[keys, :]
            if masked:
                each = width // len(starts)
                lane = lax.broadcasted_iota(jnp.int32, (1, width), 1)
                col = starts[0] + lane
                for i in range(1, len(starts)):
                    col = jnp.where(lane >= i * each, starts[i] + lane - i * each, col)
                visible = col >= lo_ref[...]
                if causal:
                    row = row0 + lax.broadcasted_iota(jnp.int32, (rows, 1), 0)
                    visible = visible & (col <= row)
            scores = []
            for u in range(UNROLL):
                q = q_ref[:, pl.ds(pl.multiple_of((t * UNROLL + u) * HEAD_DIM, HEAD_DIM), HEAD_DIM)]
                s = lax.dot_general(
                    q, k, (((1,), (1,)), ((), ())), preferred_element_type=jnp.float32
                )
                scores.append(jnp.where(visible, s, HIDDEN) if masked else s)
            for u in range(UNROLL):
                g = t * UNROLL + u
                s = scores[u]
                old = top[g]
                new = jnp.maximum(old, jnp.max(s, axis=1, keepdims=True))
                top[g] = new
                wide = jnp.concatenate([new] * (width // HEAD_DIM), axis=1)
                weights = jnp.exp2((s - wide) * EXPONENT_SCALE)
                fade = jnp.exp2((old - new) * EXPONENT_SCALE)
                summed = jnp.dot(
                    weights.astype(jnp.bfloat16), v, preferred_element_type=jnp.float32
                )
                acc[g] = acc[g] * jnp.concatenate([fade, fade], axis=1) + summed
            return 0

        lax.fori_loop(0, GROUPS // UNROLL, step, 0)

    def chunk(causal, j, _):
        one = info[base + 2 * j]
        two = info[base + 2 * j + 1]
        keys = pl.ds(pl.multiple_of(j * 2 * rows, 2 * rows), 2 * rows)
        any_seen = seen(one, rows) | seen(two, rows)
        both = whole(one, rows) & whole(two, rows)
        pl.when(any_seen & both)(lambda: work(keys, 2 * rows, [one], False))
        pl.when(any_seen & jnp.logical_not(both))(
            lambda: work(keys, 2 * rows, [one, two], True, causal)
        )
        return 0

    pairs = total // (2 * rows)
    if causal_chunks:
        lax.fori_loop(0, causal_chunks, functools.partial(chunk, True), 0)
    lax.fori_loop(causal_chunks, pairs, functools.partial(chunk, False), 0)
    extra = total - pairs * 2 * rows
    if extra:
        start = info[base + 2 * pairs]
        pl.when(seen(start, extra))(
            lambda: work(pl.ds(pairs * 2 * rows, extra), extra, [start], True)
        )
    if last:
        for g in range(GROUPS):
            out_ref[:, pl.ds(g * HEAD_DIM, HEAD_DIM)] = (
                acc[g, :, :HEAD_DIM] / acc[g, :, HEAD_DIM:]
            ).astype(jnp.bfloat16)


def attend(info, lo, q, blocks, state, base, causal_chunks, last):
    rows = q.shape[0]
    sizes = tuple(b.shape[0] for b in blocks)
    total = sum(sizes)
    first = state is None
    vmem = pl.BlockSpec(memory_space=pltpu.VMEM)
    acc = jax.ShapeDtypeStruct((GROUPS, rows, 2 * HEAD_DIM), jnp.float32)
    top = jax.ShapeDtypeStruct((GROUPS, rows, HEAD_DIM), jnp.float32)
    scratch = [
        pltpu.VMEM((total, HEAD_DIM), jnp.bfloat16),
        pltpu.VMEM((total, 2 * HEAD_DIM), jnp.bfloat16),
    ]
    if last:
        out = jax.ShapeDtypeStruct((rows, GROUPS * HEAD_DIM), jnp.bfloat16)
        out_specs = vmem
        scratch = [pltpu.VMEM(acc.shape, acc.dtype), pltpu.VMEM(top.shape, top.dtype)] + scratch
    else:
        out = (acc, top)
        out_specs = (vmem, vmem)
    args = [info, lo, q, *blocks] + ([] if first else list(state))
    return pl.pallas_call(
        functools.partial(attend_kernel, sizes, base, causal_chunks, first, last),
        out_shape=out,
        out_specs=out_specs,
        in_specs=[pl.BlockSpec(memory_space=pltpu.SMEM)] + [vmem] * (len(args) - 1),
        scratch_shapes=scratch,
        compiler_params=pltpu.CompilerParams(vmem_limit_bytes=24 << 20),
        cost_estimate=pl.CostEstimate(
            flops=4 * rows * GROUPS * total * HEAD_DIM,
            bytes_accessed=8 << 20,
            transcendentals=rows * GROUPS * total,
        ),
        name="attend",
    )(*args)


def ring(n, step):
    return [(i, (i + step) % n) for i in range(n)]


def local(queries, keys, values, doc_ids, residual, out_weight):
    tokens = queries.shape[0]
    rows = CORES * tokens
    half = queries.shape[1] // 2
    core = lax.axis_index("core")
    z = lax.axis_index("z")
    x = lax.axis_index("x")
    chip = z * X + x
    row0 = chip * rows
    is0 = core == 0

    swap = [(0, 1), (1, 0)]
    y = lax.axis_index("tp")

    def head_split(mine0, mine1):
        kept = jnp.where(is0, mine0, mine1)
        sent = jnp.where(is0, mine1, mine0)
        got = lax.ppermute(sent, "core", swap)
        return jnp.where(
            is0, jnp.concatenate([kept, got], axis=0), jnp.concatenate([got, kept], axis=0)
        )

    def kv_of(h):
        cols = slice(h * HEAD_DIM, (h + 1) * HEAD_DIM)
        return jnp.concatenate([keys[:, cols], values[:, cols]], axis=1)

    kv = head_split(kv_of(0), kv_of(1))
    q = head_split(queries[:, :half], queries[:, half:])

    begins = jnp.sum(
        (doc_ids[None, :] < jnp.arange(16, dtype=jnp.int32)[:, None]).astype(jnp.int32), axis=1
    )
    own_docs = lax.dynamic_slice_in_dim(doc_ids, row0, rows)
    lo = jnp.sum(
        jnp.where(own_docs[:, None] == jnp.arange(16, dtype=jnp.int32)[None, :], begins[None, :], 0),
        axis=1,
    )

    spots = jnp.arange(4 * (BACK + 1), dtype=jnp.int32)
    back = z - spots // 4
    aside = jnp.where(spots % 4 == 3, 2, spots % 4 + jnp.where(spots % 4 == 1, 2, 0))
    aside = jnp.where(spots % 4 == 2, 1, aside)
    starts = jnp.where(back >= 0, (back * X + (x + aside) % X) * rows, -1)
    tail_start = jnp.where(
        (x == 0) & (z > BACK), row0 - (X * BACK + 1) * rows + rows // 2, -1
    )
    info = jnp.concatenate(
        [jnp.stack([row0, lo[0], lo[rows - 1]]), starts, tail_start[None]]
    ).astype(jnp.int32)

    def forward(block, step, low):
        return lax.ppermute(block, "z", [(i, i + step) for i in range(low, Z - step)])

    def from_sides(block, left, right, far):
        return [
            lax.ppermute(block, "x", left),
            lax.ppermute(block, "x", right),
            lax.ppermute(block, "x", far),
        ]

    full = (ring(X, 1), ring(X, -1), ring(X, 2))
    pieces = [out_weight] + from_sides(out_weight, *full)
    weight = jnp.stack(
        [
            jnp.where(
                j == x,
                pieces[0],
                jnp.where(
                    j == (x + 3) % X,
                    pieces[1],
                    jnp.where(j == (x + 1) % X, pieces[2], pieces[3]),
                ),
            )
            for j in range(X)
        ]
    )
    weight = lax.all_gather(weight, "z", axis=0, tiled=False)

    lo_col = lo[:, None]
    held = kv
    blocks = None
    state = None
    for k in range(BACK + 1):
        if k == 0:
            pairs = ([(0, 1), (1, 2), (2, 3)], [(0, 3)], [(0, 2), (1, 3)])
        elif k == BACK:
            pairs = (ring(X, 1), [(1, 0), (2, 1), (3, 2)], [(2, 0), (3, 1)])
        else:
            pairs = full
        ahead = forward(held, 1, k) if k < BACK else None
        coming = [held] + from_sides(held, *pairs)
        if k == BACK:
            coming.append(
                lax.ppermute(
                    held[rows // 2 :],
                    ("z", "x"),
                    [(i * X + X - 1, (i + 1) * X) for i in range(BACK, Z - 1)],
                )
            )
        if k > 0:
            state = attend(
                info, lo_col, q, blocks, state, 3 + 4 * (k - 1), 2 if k == 1 else 0, False
            )
        if k < BACK:
            ahead, coming, state = lax.optimization_barrier((ahead, coming, state))
        held, blocks = ahead, coming
    state = attend(info, lo_col, q, blocks, state, 3 + 4 * BACK, 0, True)
    attended = state

    other = lax.ppermute(attended, "core", swap)
    attended = jnp.where(
        is0,
        jnp.concatenate([attended, other], axis=1),
        jnp.concatenate([other, attended], axis=1),
    )

    def share(d):
        block = lax.dynamic_slice_in_dim(weight, ((y + d) % TP) * 2, 2, axis=0)
        return lax.dot_general(
            attended,
            block.reshape(-1, out_weight.shape[1]),
            (((1,), (1,)), ((), ())),
            preferred_element_type=jnp.float32,
        )

    across = share(2).astype(jnp.bfloat16)
    up = lax.ppermute(across[:tokens], "tp", ring(TP, 1)).astype(jnp.float32)
    down = lax.ppermute(across[tokens:], "tp", ring(TP, -1)).astype(jnp.float32)
    after, before = share(1), share(3)
    after = jnp.concatenate([after[:tokens] + up, after[tokens:]], axis=0)
    before = jnp.concatenate([before[:tokens], before[tokens:] + down], axis=0)
    got = [
        lax.ppermute(after.astype(jnp.bfloat16), "tp", ring(TP, 1)),
        lax.ppermute(before.astype(jnp.bfloat16), "tp", ring(TP, -1)),
    ]
    mixed = share(0)
    for part in got:
        mixed = mixed + part.astype(jnp.float32)
    kept = jnp.where(is0, mixed[:tokens], mixed[tokens:])
    sent = jnp.where(is0, mixed[tokens:], mixed[:tokens]).astype(jnp.bfloat16)
    given = lax.ppermute(sent, "core", swap).astype(jnp.float32)
    even = jnp.where(is0, kept, given).reshape(tokens, -1, out_weight.shape[0])
    odd = jnp.where(is0, given, kept).reshape(tokens, -1, out_weight.shape[0])
    mixed = jnp.stack([even, odd], axis=2).reshape(residual.shape)
    return (residual.astype(jnp.float32) + mixed).astype(jnp.bfloat16)


def solution(mesh):
    mesh = Mesh(mesh.devices.reshape(Z, X, CORES, TP), ("z", "x", "core", "tp"))
    tile = P(("z", "x", "core"), "tp")
    return jax.shard_map(
        local,
        mesh=mesh,
        in_specs=(tile, tile, tile, P(), tile, tile),
        out_specs=tile,
        check_vma=False,
    )
```
